32 devices in a mesh: prompt: 8 (over y, x, core), resp: 4 (over z).
Axes of the slice: x: 2, y: 2, z: 4, core: 2. Of those that a mesh axis runs over, the one named last changes fastest.
Arguments:
- hidden_states: bfloat16 [8, 4, 256, 8192], P('prompt', 'resp'), may hold values from -6 to 6
- queries: bfloat16 [8, 4, 256, 1024], P('prompt', 'resp'), may hold values from -100 to 100
- prefix_kv: bfloat16 [8, 512, 256], P('prompt', 'resp'), may hold values from -4 to 4
- kv_weight: bfloat16 [8192, 256], replicated, may hold values from -0.0625 to 0.0625
- out_grad: bfloat16 [8, 4, 256, 1024], P('prompt', 'resp'), may hold values from -6 to 6
- lengths: int32 [8, 4], P('prompt', 'resp'), may hold values from 128 to 256, as said below
- rewards: int32 [8, 4], P('prompt', 'resp'), may hold values from 0 to 3
Outputs:
- attn_out: float32 [8, 4, 256, 1024], P('prompt', 'resp')
- grad_queries: float32 [8, 4, 256, 1024], P('prompt', 'resp')
- grad_prefix_kv: float32 [8, 512, 256], P('prompt', 'resp')
- grad_kv_weight: float32 [8192, 256], P(('prompt', 'resp'))
The draws below stay inside these ranges and needn't reach their ends.
Inputs may be any that keep to these rules, and one draw needn't show every extreme that they name: `lengths`: every length is a multiple of 16, and in every prompt some response has all 256 positions live.
All inputs are finite; a program needn't handle non-finite values.
Results may differ from the reference program's by a relative error of at most 0.029.
Values may be sent and summed in bfloat16 or wider, within the bound.
A program may use at most 128 MiB of HBM per device.

```python
import math
import jax
import jax.numpy as jnp
from jax import lax

D = 8192
HQ = 8
HD = 128
RESP = 256
PREFIX = 512
PROMPTS = 8
SAMPLES = 4


def joint_draw(key):
    key_part = jnp.clip(jax.random.normal(jax.random.fold_in(key, 11), (PROMPTS, PREFIX, HD), jnp.float32), -4.0, 4.0)
    value_part = jnp.clip(jax.random.normal(jax.random.fold_in(key, 12), (PROMPTS, PREFIX, HD), jnp.float32), -4.0, 4.0)
    query_part = jnp.clip(1.5 * jax.random.normal(jax.random.fold_in(key, 13), (PROMPTS, SAMPLES, RESP, HQ, HD), jnp.float32), -6.0, 6.0)
    return (query_part.reshape(PROMPTS, SAMPLES, RESP, HQ * HD), jnp.concatenate([key_part, value_part], axis=2))


def draw_queries(key, part):
    return joint_draw(key)[0].astype(jnp.bfloat16)


def draw_prefix_kv(key, part):
    return joint_draw(key)[1].astype(jnp.bfloat16)


def draw_lengths(key, part):
    blocks = jax.random.randint(jax.random.fold_in(key, 21), (PROMPTS, SAMPLES), RESP // 32, RESP // 16 + 1)
    full_one = jax.random.randint(jax.random.fold_in(key, 22), (PROMPTS, 1), 0, SAMPLES)
    sample_ids = lax.broadcasted_iota(jnp.int32, (PROMPTS, SAMPLES), 1)
    return (jnp.where(sample_ids == full_one, RESP // 16, blocks) * 16).astype(jnp.int32)


def with_ends(drawn, stream_key, low, largest):
    place = [jax.random.randint(jax.random.fold_in(stream_key, axis), (), 0, length) for axis, length in enumerate(drawn.shape)]
    longest = drawn.shape.index(max(drawn.shape))
    beside = place[:longest] + [(place[longest] + 1) % drawn.shape[longest]] + place[longest + 1:]
    return drawn.at[tuple(place)].set(low).at[tuple(beside)].set(largest)


def steps_of(key, extent, pieces, smallest, largest):
    level, own = 1.0, jax.random.fold_in(key, 6)
    for axis_at, shards_of in pieces:
        heights = jnp.exp(jax.random.uniform(jax.random.fold_in(own, axis_at), (shards_of,), jnp.float32, smallest / len(pieces), largest / len(pieces)))
        level = level * jnp.repeat(heights, extent[axis_at] // shards_of).reshape([-1 if axis == axis_at else 1 for axis in range(len(extent))])
    return level


def gaussian(stream_key, dims, scale, limit, shards=(), held_as=jnp.bfloat16):
    result = scale * jax.random.normal(stream_key, dims, jnp.float32)
    if shards:
        result = result * steps_of(stream_key, dims, shards, -0.22, 0.18)
    return jnp.clip(result, -limit, limit).astype(held_as)


def setup_inputs(seed: int = 0) -> dict:
    key_list = jax.random.split(jax.random.key(seed), 8)
    hidden_states = gaussian(key_list[0], (PROMPTS, SAMPLES, RESP, D), 1.0, 6.0, ((0, 8), (1, 4)))
    queries = draw_queries(jax.random.fold_in(key_list[7], 71), 0)
    prefix_kv = draw_prefix_kv(jax.random.fold_in(key_list[7], 71), 0)
    kv_weight = gaussian(key_list[3], (D, 2 * HD), D ** -0.5, 0.0625)
    out_grad = gaussian(key_list[4], (PROMPTS, SAMPLES, RESP, HQ * HD), 1.0, 6.0, ((0, 8), (1, 4)))
    lengths = draw_lengths(jax.random.fold_in(key_list[7], 71), 0)
    rewards = with_ends(jax.random.randint(key_list[6], (PROMPTS, SAMPLES), 0, 4), jax.random.fold_in(key_list[6], 1), 0, 3).astype(jnp.int32)
    return dict(hidden_states=hidden_states, queries=queries, prefix_kv=prefix_kv, kv_weight=kv_weight, out_grad=out_grad, lengths=lengths, rewards=rewards)


def one_response(query, grad_in, kv_resp, prefix, length, loss_weight):
    flat_rows = RESP * HQ
    key_rows = jnp.concatenate([prefix[:, :HD], kv_resp[:, :HD]], axis=0)
    value_rows = jnp.concatenate([prefix[:, HD:], kv_resp[:, HD:]], axis=0)
    query_rows = query.reshape(flat_rows, HD)
    position = lax.broadcasted_iota(jnp.int32, (flat_rows, 1), 0) // HQ
    key_pos = lax.broadcasted_iota(jnp.int32, (1, RESP), 1)
    allowed = jnp.concatenate([jnp.ones((flat_rows, PREFIX), dtype=bool), (key_pos <= position) & (key_pos < length)], axis=1)
    softmax_scale = 1.0 / math.sqrt(HD)
    scores = jnp.dot(query_rows, key_rows.T, preferred_element_type=jnp.float32) * softmax_scale
    scores = jnp.where(allowed, scores, -jnp.inf)
    row_max = lax.optimization_barrier(jnp.max(scores, axis=1, keepdims=True))
    log_total = row_max + jnp.log(lax.optimization_barrier(jnp.sum(jnp.exp(scores - row_max), axis=1, keepdims=True)))
    probs_full = jnp.exp(scores - log_total)
    probs = probs_full.astype(jnp.bfloat16)
    attended_full = jnp.dot(probs, value_rows, preferred_element_type=jnp.float32)
    attended = attended_full.astype(jnp.bfloat16)
    in_range = lax.broadcasted_iota(jnp.int32, (RESP, 1), 0) < length
    cotangent = jnp.where(in_range, loss_weight * grad_in.astype(jnp.float32), 0.0).astype(jnp.bfloat16)
    cotangent = cotangent.reshape(flat_rows, HD)
    row_delta = lax.optimization_barrier(jnp.sum(cotangent.astype(jnp.float32) * attended.astype(jnp.float32), axis=1, keepdims=True))
    grad_probs = jnp.dot(cotangent, value_rows.T, preferred_element_type=jnp.float32)
    grad_scores = (probs_full * (grad_probs - row_delta) * softmax_scale).astype(jnp.bfloat16)
    grad_query = jnp.dot(grad_scores, key_rows, preferred_element_type=jnp.float32)
    key_grad = jnp.dot(grad_scores.T, query_rows, preferred_element_type=jnp.float32)
    value_grad = jnp.dot(probs.T, cotangent, preferred_element_type=jnp.float32)
    both_grads = jnp.concatenate([key_grad, value_grad], axis=1)
    resp_grad = both_grads[PREFIX:].astype(jnp.bfloat16)
    return (attended_full.reshape(RESP, HQ * HD), grad_query.reshape(RESP, HQ * HD), both_grads[:PREFIX], resp_grad)

def reference(hidden_states, queries, prefix_kv, kv_weight, out_grad, lengths, rewards):
    reward = rewards.astype(jnp.float32)
    group_mean = lax.optimization_barrier(jnp.mean(reward, axis=1, keepdims=True))
    centered = reward - group_mean
    spread = jnp.sqrt(lax.optimization_barrier(jnp.mean(centered * centered, axis=1, keepdims=True)))
    advantage = centered / jnp.maximum(spread, 1.0)
    total_len = lax.optimization_barrier(jnp.sum(lengths.astype(jnp.float32), axis=1, keepdims=True))
    loss_weight = -advantage * (RESP * SAMPLES) / total_len

    def per_prompt(weight_acc, item):
        states, query_group, prefix, grads, lens, weights = item

        def per_sample(carry, inner):
            prefix_acc, weight_sum = carry
            state, query, grad_in, length, one_weight = inner
            kv_resp = jnp.dot(state, kv_weight, preferred_element_type=jnp.float32).astype(jnp.bfloat16)
            attended, grad_query, prefix_term, resp_grad = one_response(query, grad_in, kv_resp, prefix, length, one_weight)
            weight_sum = weight_sum + jnp.dot(state.T, resp_grad, preferred_element_type=jnp.float32)
            return ((prefix_acc + prefix_term, weight_sum), (attended, grad_query))
        start_acc = jnp.zeros((PREFIX, 2 * HD), jnp.float32)
        (prefix_sum, weight_acc), (attended, grad_query) = lax.scan(per_sample, (start_acc, weight_acc), (states, query_group, grads, lens, weights))
        return (weight_acc, (attended, grad_query, prefix_sum))
    start_weight = jnp.zeros((D, 2 * HD), jnp.float32)
    grad_kv_weight, (attn_out, grad_queries, grad_prefix_kv) = lax.scan(per_prompt, start_weight, (hidden_states, queries, prefix_kv, out_grad, lengths, loss_weight))
    return (attn_out, grad_queries, grad_prefix_kv, grad_kv_weight)
```

```python
import math

import jax
import jax.numpy as jnp
from jax import lax
from jax.experimental import pallas as pl
from jax.experimental.pallas import tpu as pltpu
from jax.sharding import PartitionSpec as P

F32 = jnp.float32
BF16 = jnp.bfloat16
MESH = pl.DeviceIdType.MESH
NT = (((1,), (1,)), ((), ()))
TN = (((0,), (0,)), ((), ()))


def flip(value, mask):
    out = value
    bit = 0
    while (1 << bit) <= mask:
        if (mask >> bit) & 1:
            out = out + (1 - 2 * ((value // (1 << bit)) % 2)) * (1 << bit)
        bit += 1
    return out


def make_kernel(prompts, samples, rows, heads, hd, shard, model):
    bits = (prompts // 2).bit_length() - 1
    half = prompts // 2
    chunk = model // prompts
    block = chunk // samples
    prefix = shard * samples
    scale = 1.0 / math.sqrt(hd)
    log2e = 1.0 / math.log(2.0)
    stepwise = block % 128 == 0
    orders = (list(range(bits)), list(reversed(range(bits))))

    def kernel(
        hidden, queries, prefix_in, weight, out_grad, lengths, rewards,
        attn_out, grad_queries, grad_prefix, grad_weight,
        hid, hid_other, wgt, qry, gout, kv, kv_t, stats,
        attn_v, gq_v, acc, prefix_send, prefix_recv, resp_grad, grads, z_recv, *rest,
    ):
        recv_bufs = (rest[:bits], rest[bits:2 * bits])
        (load_sem, out_sem, hx_send, hx_recv, gather_send, gather_recv, stat_send, stat_recv,
         own_sem, rg_send, rg_recv, ps_send, ps_recv, red_send, red_recv, z_send, z_recv_sem) = rest[2 * bits:]
        p = lax.axis_index("prompt")
        z = lax.axis_index("resp")
        core = p % 2
        high = p // 2
        my_bits = [(high // (1 << b)) % 2 for b in range(bits)]
        partner = {"prompt": flip(p, 1)}
        bit_peer = [{"prompt": flip(p, 2 << b)} for b in range(bits)]
        z_of = [flip(z, k) for k in range(samples)]
        z_peer = [{"resp": z_of[k]} for k in range(samples)]

        hid_loads, wgt_loads = [], []
        for j in range(prompts):
            cols = pl.ds(j * chunk, chunk)
            a = pltpu.make_async_copy(hidden.at[0, 0, :, cols], hid.at[j], load_sem.at[j])
            b = pltpu.make_async_copy(weight.at[cols], wgt.at[j], load_sem.at[prompts + j])
            a.start()
            b.start()
            hid_loads.append(a)
            wgt_loads.append(b)
        q_load = pltpu.make_async_copy(queries.at[0, 0], qry, load_sem.at[2 * prompts])
        g_load = pltpu.make_async_copy(out_grad.at[0, 0], gout, load_sem.at[2 * prompts + 1])
        own_rows = pl.ds(pl.multiple_of(z * shard, shard), shard)
        own_prefix = pltpu.make_async_copy(prefix_in.at[0], kv.at[own_rows], own_sem)
        own_prefix.start()
        q_load.start()
        g_load.start()

        row_id = lax.broadcasted_iota(jnp.int32, (8, 128), 0)
        length = lengths[0, 0]
        mine = jnp.where(row_id == 0, rewards[0, 0].astype(F32), length.astype(F32))
        stats[0] = mine

        barrier = pltpu.get_barrier_semaphore()
        peers = [partner] + bit_peer + z_peer[1:]
        for peer in peers:
            pl.semaphore_signal(barrier, inc=1, device_id=peer, device_id_type=MESH)
        pl.semaphore_wait(barrier, len(peers))

        def remote(src, dst, ssem, rsem, peer):
            return pltpu.make_async_remote_copy(
                src_ref=src, dst_ref=dst, send_sem=ssem, recv_sem=rsem,
                device_id=peer, device_id_type=MESH,
            )

        gathers, stat_copies = [], []
        for k in range(samples - 1, 0, -1):
            g = remote(prefix_in.at[0], kv.at[own_rows], gather_send.at[k], gather_recv.at[k], z_peer[k])
            s = remote(stats.at[0], stats.at[k], stat_send.at[k], stat_recv.at[k], z_peer[k])
            g.start()
            s.start()
            gathers.append(g)
            stat_copies.append(s)
        swaps = []
        for j in range(half):
            cols = pl.ds(pl.multiple_of((2 * j + 1 - core) * chunk, chunk), chunk)
            c = remote(hidden.at[0, 0, :, cols], hid_other.at[j], hx_send.at[j], hx_recv.at[j], partner)
            c.start()
            swaps.append(c)

        total = jnp.zeros((rows, 2 * hd), F32)
        for j in range(prompts):
            hid_loads[j].wait()
            wgt_loads[j].wait()
            total = total + jnp.dot(hid[j], wgt[j], preferred_element_type=F32)
        kv[prefix:, :] = total.astype(BF16)

        for s in stat_copies:
            s.wait()
        reward_sum = mine
        for k in range(1, samples):
            reward_sum = reward_sum + stats[k]
        mean = reward_sum[0:1, :] / samples
        square = jnp.zeros((1, 128), F32)
        for k in range(samples):
            d = stats[k][0:1, :] - mean
            square = square + d * d
        spread = jnp.sqrt(square / samples)
        advantage = (mine[0:1, :] - mean) / jnp.maximum(spread, 1.0)
        loss_weight = -advantage * (rows * samples) / reward_sum[1:2, :]

        own_prefix.wait()
        for g in gathers:
            g.wait()
        kv_t[...] = kv[...].astype(F32).T.astype(BF16)
        acc[...] = jnp.zeros_like(acc)
        q_load.wait()
        g_load.wait()

        live = lax.broadcasted_iota(jnp.int32, (rows, hd), 0) < length
        key_id = lax.broadcasted_iota(jnp.int32, (rows, rows), 0)
        time_id = lax.broadcasted_iota(jnp.int32, (rows, rows), 1)
        allowed = (key_id <= time_id) & (key_id < length)

        def head(h, carry):
            cols = pl.ds(pl.multiple_of(h * hd, hd), hd)
            q = qry[:, cols]
            cot32 = jnp.where(live, gout[:, cols].astype(F32) * loss_weight, 0.0)
            cot = cot32.astype(BF16)
            cot_t32 = cot.astype(F32).T
            cot_t = cot_t32.astype(BF16)
            s_pre = lax.dot_general(kv[:prefix, :hd], q, NT, preferred_element_type=F32) * (scale * log2e)
            s_res = lax.dot_general(kv[prefix:, :hd], q, NT, preferred_element_type=F32) * (scale * log2e)
            s_res = jnp.where(allowed, s_res, -jnp.inf)
            top = jnp.maximum(jnp.max(s_pre, axis=0, keepdims=True), jnp.max(s_res, axis=0, keepdims=True))
            e_pre = jnp.exp2(s_pre - top)
            e_res = jnp.exp2(s_res - top)
            inv = 1.0 / (jnp.sum(e_pre, axis=0, keepdims=True) + jnp.sum(e_res, axis=0, keepdims=True))
            f_pre = e_pre * inv
            f_res = e_res * inv
            p_pre = f_pre.astype(BF16)
            p_res = f_res.astype(BF16)
            out_t = jnp.dot(kv_t[hd:, :prefix], p_pre, preferred_element_type=F32) + jnp.dot(
                kv_t[hd:, prefix:], p_res, preferred_element_type=F32)
            attn_v[:, cols] = out_t.T
            delta = jnp.sum(cot_t32 * out_t.astype(BF16).astype(F32), axis=0, keepdims=True)
            d_pre = jnp.dot(kv[:prefix, hd:], cot_t, preferred_element_type=F32)
            d_res = jnp.dot(kv[prefix:, hd:], cot_t, preferred_element_type=F32)
            gs_pre = (f_pre * (d_pre - delta)).astype(BF16)
            gs_res = (f_res * (d_res - delta)).astype(BF16)
            gq_t = jnp.dot(kv_t[:hd, :prefix], gs_pre, preferred_element_type=F32) + jnp.dot(
                kv_t[:hd, prefix:], gs_res, preferred_element_type=F32)
            gq_v[:, cols] = (gq_t * scale).T
            acc[:prefix, :hd] += jnp.dot(gs_pre, q, preferred_element_type=F32)
            acc[prefix:, :hd] += jnp.dot(gs_res, q, preferred_element_type=F32)
            acc[:prefix, hd:] += jnp.dot(p_pre, cot, preferred_element_type=F32)
            acc[prefix:, hd:] += jnp.dot(p_res, cot, preferred_element_type=F32)
            return carry

        lax.fori_loop(0, heads, head, 0)

        resp_grad[0, :, :hd] = (acc[prefix:, :hd] * scale).astype(BF16)
        resp_grad[0, :, hd:] = acc[prefix:, hd:].astype(BF16)
        rg = remote(resp_grad.at[0], resp_grad.at[1], rg_send, rg_recv, partner)
        rg.start()
        out_copies = [
            pltpu.make_async_copy(attn_v, attn_out.at[0, 0], out_sem.at[0]),
            pltpu.make_async_copy(gq_v, grad_queries.at[0, 0], out_sem.at[1]),
        ]
        for c in out_copies:
            c.start()
        prefix_send[:, :hd] = (acc[:prefix, :hd] * scale).astype(BF16)
        prefix_send[:, hd:] = acc[:prefix, hd:].astype(BF16)
        prefix_copies = []
        for k in range(samples - 1, 0, -1):
            dest = pl.ds(pl.multiple_of(z_of[k] * shard, shard), shard)
            c = remote(prefix_send.at[dest], prefix_recv.at[k - 1], ps_send.at[k], ps_recv.at[k], z_peer[k])
            c.start()
            prefix_copies.append(c)
        for c in swaps:
            c.wait()
        rg.wait()

        def spot(s, zd, fixed):
            return (s, zd) + tuple(fixed[b] for b in reversed(range(bits)))

        def project(j, cols, width):
            mine_part = lax.dot_general(
                hid[2 * j + core, :, cols], resp_grad[0], TN, preferred_element_type=F32)
            return mine_part + lax.dot_general(
                hid_other[j, :, cols], resp_grad[1], TN, preferred_element_type=F32)

        def static_bits(j):
            return [(j >> b) & 1 for b in range(bits)]

        def produce(k):
            cols = pl.ds(pl.multiple_of(z_of[k] * block, block), block)
            for j in range(half):
                value = project(j, cols, block).astype(BF16)
                for s in range(2):
                    grads[spot(s, z_of[k], static_bits(j))] = value[:, s * hd:(s + 1) * hd]

        if not stepwise:
            for j in range(half):
                value = project(j, pl.ds(0, chunk), chunk).astype(BF16)
                for zd in range(samples):
                    for s in range(2):
                        grads[spot(s, zd, static_bits(j))] = value[zd * block:(zd + 1) * block, s * hd:(s + 1) * hd]

        started = {}

        def kept(s, phase):
            fixed = [slice(None)] * bits
            for b in orders[s][:phase]:
                fixed[b] = my_bits[b]
            return fixed

        def send(k, phase):
            for s in range(2):
                b = orders[s][phase]
                fixed = kept(s, phase)
                fixed[b] = 1 - my_bits[b]
                c = remote(
                    grads.at[spot(s, z_of[k], fixed)], recv_bufs[s][phase].at[k],
                    red_send.at[s, phase, k], red_recv.at[s, phase, k], bit_peer[b])
                c.start()
                started[s, phase, k] = c

        def merge(k, phase):
            for s in range(2):
                started[s, phase, k].wait_recv()
                at = spot(s, z_of[k], kept(s, phase + 1))
                grads[at] = (grads[at].astype(F32) + recv_bufs[s][phase][k].astype(F32)).astype(BF16)

        z_copies = []

        def send_z(k):
            if k == 0:
                return
            for s in range(2):
                c = remote(
                    grads.at[spot(s, z_of[k], my_bits)], z_recv.at[s, k - 1],
                    z_send.at[s, k], z_recv_sem.at[s, k], z_peer[k])
                c.start()
                z_copies.append(c)

        steps = list(range(samples - 1, -1, -1))
        ahead = 1
        for tick in range(samples + ahead + bits):
            if tick < samples:
                if stepwise:
                    produce(steps[tick])
                send(steps[tick], 0)
            for phase in range(bits):
                at = tick - ahead - phase
                if 0 <= at < samples:
                    merge(steps[at], phase)
                    if phase + 1 < bits:
                        send(steps[at], phase + 1)
                    else:
                        send_z(steps[at])

        for c in prefix_copies:
            c.wait()
        own_sum = acc[own_rows, :hd] * scale
        own_val = acc[own_rows, hd:]
        for k in range(samples - 1):
            own_sum = own_sum + prefix_recv[k, :, :hd].astype(F32)
            own_val = own_val + prefix_recv[k, :, hd:].astype(F32)
        grad_prefix[0, :, :hd] = own_sum
        grad_prefix[0, :, hd:] = own_val

        for c in z_copies:
            c.wait()
        for s in range(2):
            value = grads[spot(s, z, my_bits)].astype(F32)
            for k in range(samples - 1):
                value = value + z_recv[s, k].astype(F32)
            grad_weight[:, s * hd:(s + 1) * hd] = value
        for c in started.values():
            c.wait_send()
        for c in out_copies:
            c.wait()

    keys = prefix + rows
    dma = pltpu.SemaphoreType.DMA
    reduce_bufs = [
        pltpu.VMEM((samples,) + (2,) * (bits - 1 - phase) + (block, hd), BF16)
        for _ in range(2) for phase in range(bits)
    ]
    scratch = [
        pltpu.VMEM((prompts, rows, chunk), BF16),
        pltpu.VMEM((half, rows, chunk), BF16),
        pltpu.VMEM((prompts, chunk, 2 * hd), BF16),
        pltpu.VMEM((rows, heads * hd), BF16),
        pltpu.VMEM((rows, heads * hd), BF16),
        pltpu.VMEM((keys, 2 * hd), BF16),
        pltpu.VMEM((2 * hd, keys), BF16),
        pltpu.VMEM((samples, 8, 128), F32),
        pltpu.VMEM((rows, heads * hd), F32),
        pltpu.VMEM((rows, heads * hd), F32),
        pltpu.VMEM((keys, 2 * hd), F32),
        pltpu.VMEM((prefix, 2 * hd), BF16),
        pltpu.VMEM((samples - 1, shard, 2 * hd), BF16),
        pltpu.VMEM((2, rows, 2 * hd), BF16),
        pltpu.VMEM((2, samples) + (2,) * bits + (block, hd), BF16),
        pltpu.VMEM((2, samples - 1, block, hd), BF16),
        *reduce_bufs,
        dma((2 * prompts + 2,)), dma((2,)), dma((half,)), dma((half,)),
        dma((samples,)), dma((samples,)), dma((samples,)), dma((samples,)),
        dma, dma, dma, dma((samples,)), dma((samples,)),
        dma((2, bits, samples)), dma((2, bits, samples)), dma((2, samples)), dma((2, samples)),
    ]
    anywhere = pl.BlockSpec(memory_space=pl.ANY)
    smem = pl.BlockSpec(memory_space=pltpu.SMEM)
    vmem = pl.BlockSpec(memory_space=pltpu.VMEM)
    flops = 4 * rows * model * 2 * hd + 14 * rows * heads * keys * hd
    return pl.pallas_call(
        kernel,
        out_shape=(
            jax.ShapeDtypeStruct((1, 1, rows, heads * hd), F32),
            jax.ShapeDtypeStruct((1, 1, rows, heads * hd), F32),
            jax.ShapeDtypeStruct((1, shard, 2 * hd), F32),
            jax.ShapeDtypeStruct((block, 2 * hd), F32),
        ),
        in_specs=[anywhere] * 5 + [smem] * 2,
        out_specs=(anywhere, anywhere, vmem, vmem),
        scratch_shapes=scratch,
        compiler_params=pltpu.CompilerParams(
            collective_id=0, has_side_effects=True, vmem_limit_bytes=56 * 1024 * 1024),
        cost_estimate=pl.CostEstimate(
            flops=flops, bytes_accessed=16 * 1024 * 1024, transcendentals=rows * heads * keys),
    )


def solution(mesh):
    prompts, samples = mesh.shape["prompt"], mesh.shape["resp"]

    def on_device(hidden, queries, prefix_kv, weight, out_grad, lengths, rewards):
        hd = weight.shape[1] // 2
        call = make_kernel(
            prompts, samples, hidden.shape[2], queries.shape[3] // hd, hd, prefix_kv.shape[1], weight.shape[0])
        return call(hidden, queries, prefix_kv, weight, out_grad, lengths, rewards)

    placed = P("prompt", "resp", None, None)
    return jax.shard_map(
        on_device,
        mesh=mesh,
        in_specs=(placed, placed, P("prompt", "resp", None), P(), placed, P("prompt", "resp"), P("prompt", "resp")),
        out_specs=(placed, placed, P("prompt", "resp", None), P(("prompt", "resp"), None)),
        check_vma=False,
    )
```

```python
import math

import jax
import jax.numpy as jnp
from jax import lax
from jax.experimental import pallas as pl
from jax.experimental.pallas import tpu as pltpu
from jax.sharding import PartitionSpec as P

F32 = jnp.float32
BF16 = jnp.bfloat16
MESH = pl.DeviceIdType.MESH
NT = (((1,), (1,)), ((), ()))
TN = (((0,), (0,)), ((), ()))


def flip(value, mask):
    out = value
    bit = 0
    while (1 << bit) <= mask:
        if (mask >> bit) & 1:
            out = out + (1 - 2 * ((value // (1 << bit)) % 2)) * (1 << bit)
        bit += 1
    return out


def make_kernel(prompts, samples, rows, heads, hd, shard, model):
    bits = (prompts // 2).bit_length() - 1
    half = prompts // 2
    chunk = model // prompts
    block = chunk // samples
    prefix = shard * samples
    scale = 1.0 / math.sqrt(hd)
    log2e = 1.0 / math.log(2.0)
    stepwise = block % 128 == 0
    orders = (list(range(bits)), list(reversed(range(bits))))

    def kernel(
        hidden, queries, prefix_in, weight, out_grad, lengths, rewards,
        attn_out, grad_queries, grad_prefix, grad_weight,
        hid, hid_other, wgt, qry, gout, kv, kv_t, stats,
        attn_v, gq_v, acc, prefix_send, prefix_recv, resp_grad, grads, z_recv, *rest,
    ):
        recv_bufs = (rest[:bits], rest[bits:2 * bits])
        (load_sem, out_sem, hx_send, hx_recv, gather_send, gather_recv, stat_send, stat_recv,
         own_sem, rg_send, rg_recv, ps_send, ps_recv, red_send, red_recv, z_send, z_recv_sem) = rest[2 * bits:]
        p = lax.axis_index("prompt")
        z = lax.axis_index("resp")
        core = p % 2
        high = p // 2
        my_bits = [(high // (1 << b)) % 2 for b in range(bits)]
        partner = {"prompt": flip(p, 1)}
        bit_peer = [{"prompt": flip(p, 2 << b)} for b in range(bits)]
        z_of = [flip(z, k) for k in range(samples)]
        z_peer = [{"resp": z_of[k]} for k in range(samples)]

        hid_loads, wgt_loads = [], []
        for j in range(prompts):
            cols = pl.ds(j * chunk, chunk)
            a = pltpu.make_async_copy(hidden.at[0, 0, :, cols], hid.at[j], load_sem.at[j])
            b = pltpu.make_async_copy(weight.at[cols], wgt.at[j], load_sem.at[prompts + j])
            a.start()
            b.start()
            hid_loads.append(a)
            wgt_loads.append(b)
        q_load = pltpu.make_async_copy(queries.at[0, 0], qry, load_sem.at[2 * prompts])
        g_load = pltpu.make_async_copy(out_grad.at[0, 0], gout, load_sem.at[2 * prompts + 1])
        own_rows = pl.ds(pl.multiple_of(z * shard, shard), shard)
        own_prefix = pltpu.make_async_copy(prefix_in.at[0], kv.at[own_rows], own_sem)
        own_prefix.start()
        q_load.start()
        g_load.start()

        row_id = lax.broadcasted_iota(jnp.int32, (8, 128), 0)
        length = lengths[0, 0]
        mine = jnp.where(row_id == 0, rewards[0, 0].astype(F32), length.astype(F32))
        stats[0] = mine

        barrier = pltpu.get_barrier_semaphore()
        peers = [partner] + bit_peer + z_peer[1:]
        for peer in peers:
            pl.semaphore_signal(barrier, inc=1, device_id=peer, device_id_type=MESH)
        pl.semaphore_wait(barrier, len(peers))

        def remote(src, dst, ssem, rsem, peer):
            return pltpu.make_async_remote_copy(
                src_ref=src, dst_ref=dst, send_sem=ssem, recv_sem=rsem,
                device_id=peer, device_id_type=MESH,
            )

        gathers, stat_copies = [], []
        for k in range(samples - 1, 0, -1):
            g = remote(prefix_in.at[0], kv.at[own_rows], gather_send.at[k], gather_recv.at[k], z_peer[k])
            s = remote(stats.at[0], stats.at[k], stat_send.at[k], stat_recv.at[k], z_peer[k])
            g.start()
            s.start()
            gathers.append(g)
            stat_copies.append(s)
        swaps = []
        for j in range(half):
            cols = pl.ds(pl.multiple_of((2 * j + 1 - core) * chunk, chunk), chunk)
            c = remote(hidden.at[0, 0, :, cols], hid_other.at[j], hx_send.at[j], hx_recv.at[j], partner)
            c.start()
            swaps.append(c)

        total = jnp.zeros((rows, 2 * hd), F32)
        for j in range(prompts):
            hid_loads[j].wait()
            wgt_loads[j].wait()
            total = total + jnp.dot(hid[j], wgt[j], preferred_element_type=F32)
        kv[prefix:, :] = total.astype(BF16)

        for s in stat_copies:
            s.wait()
        reward_sum = mine
        for k in range(1, samples):
            reward_sum = reward_sum + stats[k]
        mean = reward_sum[0:1, :] / samples
        square = jnp.zeros((1, 128), F32)
        for k in range(samples):
            d = stats[k][0:1, :] - mean
            square = square + d * d
        spread = jnp.sqrt(square / samples)
        advantage = (mine[0:1, :] - mean) / jnp.maximum(spread, 1.0)
        loss_weight = -advantage * (rows * samples) / reward_sum[1:2, :]

        own_prefix.wait()
        for g in gathers:
            g.wait()
        kv_t[...] = kv[...].astype(F32).T.astype(BF16)
        acc[...] = jnp.zeros_like(acc)
        q_load.wait()
        g_load.wait()

        live = lax.broadcasted_iota(jnp.int32, (rows, hd), 0) < length
        key_id = lax.broadcasted_iota(jnp.int32, (rows, rows), 0)
        time_id = lax.broadcasted_iota(jnp.int32, (rows, rows), 1)
        allowed = (key_id <= time_id) & (key_id < length)

        def head(h, carry):
            cols = pl.ds(pl.multiple_of(h * hd, hd), hd)
            q = qry[:, cols]
            cot32 = jnp.where(live, gout[:, cols].astype(F32) * loss_weight, 0.0)
            cot = cot32.astype(BF16)
            cot_t32 = cot.astype(F32).T
            cot_t = cot_t32.astype(BF16)
            s_pre = lax.dot_general(kv[:prefix, :hd], q, NT, preferred_element_type=F32) * (scale * log2e)
            s_res = lax.dot_general(kv[prefix:, :hd], q, NT, preferred_element_type=F32) * (scale * log2e)
            s_res = jnp.where(allowed, s_res, -jnp.inf)
            top = jnp.maximum(jnp.max(s_pre, axis=0, keepdims=True), jnp.max(s_res, axis=0, keepdims=True))
            e_pre = jnp.exp2(s_pre - top)
            e_res = jnp.exp2(s_res - top)
            inv = 1.0 / (jnp.sum(e_pre, axis=0, keepdims=True) + jnp.sum(e_res, axis=0, keepdims=True))
            f_pre = e_pre * inv
            f_res = e_res * inv
            p_pre = f_pre.astype(BF16)
            p_res = f_res.astype(BF16)
            out_t = jnp.dot(kv_t[hd:, :prefix], p_pre, preferred_element_type=F32) + jnp.dot(
                kv_t[hd:, prefix:], p_res, preferred_element_type=F32)
            attn_v[:, cols] = out_t.T
            delta = jnp.sum(cot_t32 * out_t.astype(BF16).astype(F32), axis=0, keepdims=True)
            d_pre = jnp.dot(kv[:prefix, hd:], cot_t, preferred_element_type=F32)
            d_res = jnp.dot(kv[prefix:, hd:], cot_t, preferred_element_type=F32)
            gs_pre = (f_pre * (d_pre - delta)).astype(BF16)
            gs_res = (f_res * (d_res - delta)).astype(BF16)
            gq_t = jnp.dot(kv_t[:hd, :prefix], gs_pre, preferred_element_type=F32) + jnp.dot(
                kv_t[:hd, prefix:], gs_res, preferred_element_type=F32)
            gq_v[:, cols] = (gq_t * scale).T
            acc[:prefix, :hd] += jnp.dot(gs_pre, q, preferred_element_type=F32)
            acc[prefix:, :hd] += jnp.dot(gs_res, q, preferred_element_type=F32)
            acc[:prefix, hd:] += jnp.dot(p_pre, cot, preferred_element_type=F32)
            acc[prefix:, hd:] += jnp.dot(p_res, cot, preferred_element_type=F32)
            return carry

        lax.fori_loop(0, heads, head, 0, unroll=4)

        resp_grad[0, :, :hd] = (acc[prefix:, :hd] * scale).astype(BF16)
        resp_grad[0, :, hd:] = acc[prefix:, hd:].astype(BF16)
        rg = remote(resp_grad.at[0], resp_grad.at[1], rg_send, rg_recv, partner)
        rg.start()
        out_copies = [
            pltpu.make_async_copy(attn_v, attn_out.at[0, 0], out_sem.at[0]),
            pltpu.make_async_copy(gq_v, grad_queries.at[0, 0], out_sem.at[1]),
        ]
        for c in out_copies:
            c.start()
        prefix_send[:, :hd] = (acc[:prefix, :hd] * scale).astype(BF16)
        prefix_send[:, hd:] = acc[:prefix, hd:].astype(BF16)
        prefix_copies = []
        for k in range(samples - 1, 0, -1):
            dest = pl.ds(pl.multiple_of(z_of[k] * shard, shard), shard)
            c = remote(prefix_send.at[dest], prefix_recv.at[k - 1], ps_send.at[k], ps_recv.at[k], z_peer[k])
            c.start()
            prefix_copies.append(c)
        for c in swaps:
            c.wait()
        rg.wait()

        def spot(s, zd, fixed):
            return (s, zd) + tuple(fixed[b] for b in reversed(range(bits)))

        def project(j, cols, width):
            mine_part = lax.dot_general(
                hid[2 * j + core, :, cols], resp_grad[0], TN, preferred_element_type=F32)
            return mine_part + lax.dot_general(
                hid_other[j, :, cols], resp_grad[1], TN, preferred_element_type=F32)

        def static_bits(j):
            return [(j >> b) & 1 for b in range(bits)]

        def produce(k):
            cols = pl.ds(pl.multiple_of(z_of[k] * block, block), block)
            for j in range(half):
                value = project(j, cols, block).astype(BF16)
                for s in range(2):
                    grads[spot(s, z_of[k], static_bits(j))] = value[:, s * hd:(s + 1) * hd]

        if not stepwise:
            for j in range(half):
                value = project(j, pl.ds(0, chunk), chunk).astype(BF16)
                for zd in range(samples):
                    for s in range(2):
                        grads[spot(s, zd, static_bits(j))] = value[zd * block:(zd + 1) * block, s * hd:(s + 1) * hd]

        started = {}

        def kept(s, phase):
            fixed = [slice(None)] * bits
            for b in orders[s][:phase]:
                fixed[b] = my_bits[b]
            return fixed

        def send(k, phase):
            for s in range(2):
                b = orders[s][phase]
                fixed = kept(s, phase)
                fixed[b] = 1 - my_bits[b]
                c = remote(
                    grads.at[spot(s, z_of[k], fixed)], recv_bufs[s][phase].at[k],
                    red_send.at[s, phase, k], red_recv.at[s, phase, k], bit_peer[b])
                c.start()
                started[s, phase, k] = c

        def merge(k, phase):
            for s in range(2):
                started[s, phase, k].wait_recv()
                at = spot(s, z_of[k], kept(s, phase + 1))
                grads[at] = (grads[at].astype(F32) + recv_bufs[s][phase][k].astype(F32)).astype(BF16)

        z_copies = []

        def send_z(k):
            if k == 0:
                return
            for s in range(2):
                c = remote(
                    grads.at[spot(s, z_of[k], my_bits)], z_recv.at[s, k - 1],
                    z_send.at[s, k], z_recv_sem.at[s, k], z_peer[k])
                c.start()
                z_copies.append(c)

        steps = list(range(samples - 1, -1, -1))
        ahead = 1
        for tick in range(samples + ahead + bits):
            if tick < samples:
                if stepwise:
                    produce(steps[tick])
                send(steps[tick], 0)
            for phase in range(bits):
                at = tick - ahead - phase
                if 0 <= at < samples:
                    merge(steps[at], phase)
                    if phase + 1 < bits:
                        send(steps[at], phase + 1)
                    else:
                        send_z(steps[at])

        for c in prefix_copies:
            c.wait()
        own_sum = acc[own_rows, :hd] * scale
        own_val = acc[own_rows, hd:]
        for k in range(samples - 1):
            own_sum = own_sum + prefix_recv[k, :, :hd].astype(F32)
            own_val = own_val + prefix_recv[k, :, hd:].astype(F32)
        grad_prefix[0, :, :hd] = own_sum
        grad_prefix[0, :, hd:] = own_val

        for c in z_copies:
            c.wait()
        for s in range(2):
            value = grads[spot(s, z, my_bits)].astype(F32)
            for k in range(samples - 1):
                value = value + z_recv[s, k].astype(F32)
            grad_weight[:, s * hd:(s + 1) * hd] = value
        for c in started.values():
            c.wait_send()
        for c in out_copies:
            c.wait()

    keys = prefix + rows
    dma = pltpu.SemaphoreType.DMA
    reduce_bufs = [
        pltpu.VMEM((samples,) + (2,) * (bits - 1 - phase) + (block, hd), BF16)
        for _ in range(2) for phase in range(bits)
    ]
    scratch = [
        pltpu.VMEM((prompts, rows, chunk), BF16),
        pltpu.VMEM((half, rows, chunk), BF16),
        pltpu.VMEM((prompts, chunk, 2 * hd), BF16),
        pltpu.VMEM((rows, heads * hd), BF16),
        pltpu.VMEM((rows, heads * hd), BF16),
        pltpu.VMEM((keys, 2 * hd), BF16),
        pltpu.VMEM((2 * hd, keys), BF16),
        pltpu.VMEM((samples, 8, 128), F32),
        pltpu.VMEM((rows, heads * hd), F32),
        pltpu.VMEM((rows, heads * hd), F32),
        pltpu.VMEM((keys, 2 * hd), F32),
        pltpu.VMEM((prefix, 2 * hd), BF16),
        pltpu.VMEM((samples - 1, shard, 2 * hd), BF16),
        pltpu.VMEM((2, rows, 2 * hd), BF16),
        pltpu.VMEM((2, samples) + (2,) * bits + (block, hd), BF16),
        pltpu.VMEM((2, samples - 1, block, hd), BF16),
        *reduce_bufs,
        dma((2 * prompts + 2,)), dma((2,)), dma((half,)), dma((half,)),
        dma((samples,)), dma((samples,)), dma((samples,)), dma((samples,)),
        dma, dma, dma, dma((samples,)), dma((samples,)),
        dma((2, bits, samples)), dma((2, bits, samples)), dma((2, samples)), dma((2, samples)),
    ]
    anywhere = pl.BlockSpec(memory_space=pl.ANY)
    smem = pl.BlockSpec(memory_space=pltpu.SMEM)
    vmem = pl.BlockSpec(memory_space=pltpu.VMEM)
    flops = 4 * rows * model * 2 * hd + 14 * rows * heads * keys * hd
    return pl.pallas_call(
        kernel,
        out_shape=(
            jax.ShapeDtypeStruct((1, 1, rows, heads * hd), F32),
            jax.ShapeDtypeStruct((1, 1, rows, heads * hd), F32),
            jax.ShapeDtypeStruct((1, shard, 2 * hd), F32),
            jax.ShapeDtypeStruct((block, 2 * hd), F32),
        ),
        in_specs=[anywhere] * 5 + [smem] * 2,
        out_specs=(anywhere, anywhere, vmem, vmem),
        scratch_shapes=scratch,
        compiler_params=pltpu.CompilerParams(
            collective_id=0, has_side_effects=True, vmem_limit_bytes=56 * 1024 * 1024),
        cost_estimate=pl.CostEstimate(
            flops=flops, bytes_accessed=16 * 1024 * 1024, transcendentals=rows * heads * keys),
    )


def hand_out(arrays, pieces=2):
    def kernel(*refs):
        count = len(arrays)
        ins, outs, held, sem = refs[:count], refs[count:2 * count], refs[2 * count:3 * count], refs[3 * count]
        loads, stores = [], []
        for i in range(count):
            axis = len(ins[i].shape) - 2
            step = ins[i].shape[axis] // pieces
            for j in range(pieces):
                at = (0,) * axis + (pl.ds(j * step, step),)
                loads.append(pltpu.make_async_copy(ins[i].at[at], held[i].at[at], sem.at[0, i, j]))
                stores.append(pltpu.make_async_copy(held[i].at[at], outs[i].at[at], sem.at[1, i, j]))
        for c in loads:
            c.start()
        for load, store in zip(loads, stores):
            load.wait()
            store.start()
        for c in stores:
            c.wait()

    anywhere = pl.BlockSpec(memory_space=pl.ANY)
    size = sum(a.size * 4 for a in arrays)
    return pl.pallas_call(
        kernel,
        out_shape=tuple(jax.ShapeDtypeStruct(a.shape, a.dtype) for a in arrays),
        in_specs=[anywhere] * len(arrays),
        out_specs=(anywhere,) * len(arrays),
        scratch_shapes=[pltpu.VMEM(a.shape, a.dtype) for a in arrays]
        + [pltpu.SemaphoreType.DMA((2, len(arrays), pieces))],
        compiler_params=pltpu.CompilerParams(vmem_limit_bytes=60 * 1024 * 1024),
        cost_estimate=pl.CostEstimate(flops=0, bytes_accessed=2 * size, transcendentals=0),
    )(*arrays)


def solution(mesh):
    prompts, samples = mesh.shape["prompt"], mesh.shape["resp"]

    def on_device(hidden, queries, prefix_kv, weight, out_grad, lengths, rewards):
        hd = weight.shape[1] // 2
        call = make_kernel(
            prompts, samples, hidden.shape[2], queries.shape[3] // hd, hd, prefix_kv.shape[1], weight.shape[0])
        return tuple(hand_out(call(hidden, queries, prefix_kv, weight, out_grad, lengths, rewards)))

    placed = P("prompt", "resp", None, None)
    return jax.shard_map(
        on_device,
        mesh=mesh,
        in_specs=(placed, placed, P("prompt", "resp", None), P(), placed, P("prompt", "resp"), P("prompt", "resp")),
        out_specs=(placed, placed, P("prompt", "resp", None), P(("prompt", "resp"), None)),
        check_vma=False,
    )
```

```python
import math

import jax
import jax.numpy as jnp
from jax import lax
from jax.experimental import pallas as pl
from jax.experimental.pallas import tpu as pltpu
from jax.sharding import PartitionSpec as P

F32 = jnp.float32
BF16 = jnp.bfloat16
MESH = pl.DeviceIdType.MESH
NT = (((1,), (1,)), ((), ()))
TN = (((0,), (0,)), ((), ()))


def flip(value, mask):
    out = value
    bit = 0
    while (1 << bit) <= mask:
        if (mask >> bit) & 1:
            out = out + (1 - 2 * ((value // (1 << bit)) % 2)) * (1 << bit)
        bit += 1
    return out


def make_kernel(prompts, samples, rows, heads, hd, shard, model):
    bits = (prompts // 2).bit_length() - 1
    half = prompts // 2
    chunk = model // prompts
    block = chunk // samples
    prefix = shard * samples
    scale = 1.0 / math.sqrt(hd)
    log2e = 1.0 / math.log(2.0)
    stepwise = block % 128 == 0
    orders = (list(range(bits)), list(reversed(range(bits))))

    def kernel(
        hidden, queries, prefix_in, weight, out_grad, lengths, rewards,
        attn_out, grad_queries, grad_prefix, grad_weight,
        hid, hid_other, wgt, qry, gout, kv, kv_t, stats,
        attn_v, gq_v, acc, prefix_send, prefix_recv, resp_grad, grads, z_recv, cots_t, own_s, own_d, *rest,
    ):
        recv_bufs = (rest[:bits], rest[bits:2 * bits])
        (load_sem, out_sem, hx_send, hx_recv, gather_send, gather_recv, stat_send, stat_recv,
         own_sem, rg_send, rg_recv, ps_send, ps_recv, red_send, red_recv, z_send, z_recv_sem) = rest[2 * bits:]
        p = lax.axis_index("prompt")
        z = lax.axis_index("resp")
        core = p % 2
        high = p // 2
        my_bits = [(high // (1 << b)) % 2 for b in range(bits)]
        partner = {"prompt": flip(p, 1)}
        bit_peer = [{"prompt": flip(p, 2 << b)} for b in range(bits)]
        z_of = [flip(z, k) for k in range(samples)]
        z_peer = [{"resp": z_of[k]} for k in range(samples)]

        hid_loads, wgt_loads = [], []
        for j in range(prompts):
            cols = pl.ds(j * chunk, chunk)
            a = pltpu.make_async_copy(hidden.at[0, 0, :, cols], hid.at[j], load_sem.at[j])
            b = pltpu.make_async_copy(weight.at[cols], wgt.at[j], load_sem.at[prompts + j])
            a.start()
            b.start()
            hid_loads.append(a)
            wgt_loads.append(b)
        q_load = pltpu.make_async_copy(queries.at[0, 0], qry, load_sem.at[2 * prompts])
        g_load = pltpu.make_async_copy(out_grad.at[0, 0], gout, load_sem.at[2 * prompts + 1])
        own_rows = pl.ds(pl.multiple_of(z * shard, shard), shard)
        own_prefix = pltpu.make_async_copy(prefix_in.at[0], kv.at[own_rows], own_sem)
        own_prefix.start()
        q_load.start()
        g_load.start()

        row_id = lax.broadcasted_iota(jnp.int32, (8, 128), 0)
        length = lengths[0, 0]
        mine = jnp.where(row_id == 0, rewards[0, 0].astype(F32), length.astype(F32))
        stats[0] = mine

        barrier = pltpu.get_barrier_semaphore()
        peers = [partner] + bit_peer + z_peer[1:]
        for peer in peers:
            pl.semaphore_signal(barrier, inc=1, device_id=peer, device_id_type=MESH)
        pl.semaphore_wait(barrier, len(peers))

        def remote(src, dst, ssem, rsem, peer):
            return pltpu.make_async_remote_copy(
                src_ref=src, dst_ref=dst, send_sem=ssem, recv_sem=rsem,
                device_id=peer, device_id_type=MESH,
            )

        gathers, stat_copies = [], []
        for k in range(samples - 1, 0, -1):
            g = remote(prefix_in.at[0], kv.at[own_rows], gather_send.at[k], gather_recv.at[k], z_peer[k])
            s = remote(stats.at[0], stats.at[k], stat_send.at[k], stat_recv.at[k], z_peer[k])
            g.start()
            s.start()
            gathers.append(g)
            stat_copies.append(s)
        swaps = []
        for j in range(half):
            cols = pl.ds(pl.multiple_of((2 * j + 1 - core) * chunk, chunk), chunk)
            c = remote(hidden.at[0, 0, :, cols], hid_other.at[j], hx_send.at[j], hx_recv.at[j], partner)
            c.start()
            swaps.append(c)

        total = jnp.zeros((rows, 2 * hd), F32)
        for j in range(prompts):
            hid_loads[j].wait()
            wgt_loads[j].wait()
            total = total + jnp.dot(hid[j], wgt[j], preferred_element_type=F32)
        kv[prefix:, :] = total.astype(BF16)

        for s in stat_copies:
            s.wait()
        reward_sum = mine
        for k in range(1, samples):
            reward_sum = reward_sum + stats[k]
        mean = reward_sum[0:1, :] / samples
        square = jnp.zeros((1, 128), F32)
        for k in range(samples):
            d = stats[k][0:1, :] - mean
            square = square + d * d
        spread = jnp.sqrt(square / samples)
        advantage = (mine[0:1, :] - mean) / jnp.maximum(spread, 1.0)
        loss_weight = -advantage * (rows * samples) / reward_sum[1:2, :]

        q_load.wait()
        g_load.wait()

        live = lax.broadcasted_iota(jnp.int32, (rows, hd), 0) < length
        key_id = lax.broadcasted_iota(jnp.int32, (rows, rows), 0)
        time_id = lax.broadcasted_iota(jnp.int32, (rows, rows), 1)
        allowed = (key_id <= time_id) & (key_id < length)

        def own_scores(h, carry):
            cols = pl.ds(pl.multiple_of(h * hd, hd), hd)
            cot = jnp.where(live, gout[:, cols].astype(F32) * loss_weight, 0.0).astype(BF16)
            cot_t = cot.astype(F32).T.astype(BF16)
            gout[:, cols] = cot
            cots_t[h] = cot_t
            s_res = lax.dot_general(kv[prefix:, :hd], qry[:, cols], NT, preferred_element_type=F32) * (scale * log2e)
            own_s[h] = jnp.where(allowed, s_res, -jnp.inf)
            own_d[h] = jnp.dot(kv[prefix:, hd:], cot_t, preferred_element_type=F32)
            return carry

        lax.fori_loop(0, heads, own_scores, 0, unroll=4)

        own_prefix.wait()
        for g in gathers:
            g.wait()
        kv_t[...] = kv[...].astype(F32).T.astype(BF16)
        acc[...] = jnp.zeros_like(acc)
        def head(h, carry):
            cols = pl.ds(pl.multiple_of(h * hd, hd), hd)
            q = qry[:, cols]
            cot = gout[:, cols]
            cot_t = cots_t[h]
            s_pre = lax.dot_general(kv[:prefix, :hd], q, NT, preferred_element_type=F32) * (scale * log2e)
            s_res = own_s[h]
            top = jnp.maximum(jnp.max(s_pre, axis=0, keepdims=True), jnp.max(s_res, axis=0, keepdims=True))
            e_pre = jnp.exp2(s_pre - top)
            e_res = jnp.exp2(s_res - top)
            inv = 1.0 / (jnp.sum(e_pre, axis=0, keepdims=True) + jnp.sum(e_res, axis=0, keepdims=True))
            f_pre = e_pre * inv
            f_res = e_res * inv
            p_pre = f_pre.astype(BF16)
            p_res = f_res.astype(BF16)
            out_t = jnp.dot(kv_t[hd:, :prefix], p_pre, preferred_element_type=F32) + jnp.dot(
                kv_t[hd:, prefix:], p_res, preferred_element_type=F32)
            attn_v[:, cols] = out_t.T
            delta = jnp.sum(cot_t.astype(F32) * out_t.astype(BF16).astype(F32), axis=0, keepdims=True)
            d_pre = jnp.dot(kv[:prefix, hd:], cot_t, preferred_element_type=F32)
            d_res = own_d[h]
            gs_pre = (f_pre * (d_pre - delta)).astype(BF16)
            gs_res = (f_res * (d_res - delta)).astype(BF16)
            gq_t = jnp.dot(kv_t[:hd, :prefix], gs_pre, preferred_element_type=F32) + jnp.dot(
                kv_t[:hd, prefix:], gs_res, preferred_element_type=F32)
            gq_v[:, cols] = (gq_t * scale).T
            acc[:prefix, :hd] += jnp.dot(gs_pre, q, preferred_element_type=F32)
            acc[prefix:, :hd] += jnp.dot(gs_res, q, preferred_element_type=F32)
            acc[:prefix, hd:] += jnp.dot(p_pre, cot, preferred_element_type=F32)
            acc[prefix:, hd:] += jnp.dot(p_res, cot, preferred_element_type=F32)
            return carry

        lax.fori_loop(0, heads, head, 0, unroll=4)

        resp_grad[0, :, :hd] = (acc[prefix:, :hd] * scale).astype(BF16)
        resp_grad[0, :, hd:] = acc[prefix:, hd:].astype(BF16)
        rg = remote(resp_grad.at[0], resp_grad.at[1], rg_send, rg_recv, partner)
        rg.start()
        out_copies = [
            pltpu.make_async_copy(attn_v, attn_out.at[0, 0], out_sem.at[0]),
            pltpu.make_async_copy(gq_v, grad_queries.at[0, 0], out_sem.at[1]),
        ]
        for c in out_copies:
            c.start()
        prefix_send[:, :hd] = (acc[:prefix, :hd] * scale).astype(BF16)
        prefix_send[:, hd:] = acc[:prefix, hd:].astype(BF16)
        prefix_copies = []
        for k in range(samples - 1, 0, -1):
            dest = pl.ds(pl.multiple_of(z_of[k] * shard, shard), shard)
            c = remote(prefix_send.at[dest], prefix_recv.at[k - 1], ps_send.at[k], ps_recv.at[k], z_peer[k])
            c.start()
            prefix_copies.append(c)
        for c in swaps:
            c.wait()
        rg.wait()

        def spot(s, zd, fixed):
            return (s, zd) + tuple(fixed[b] for b in reversed(range(bits)))

        def project(j, cols, width):
            mine_part = lax.dot_general(
                hid[2 * j + core, :, cols], resp_grad[0], TN, preferred_element_type=F32)
            return mine_part + lax.dot_general(
                hid_other[j, :, cols], resp_grad[1], TN, preferred_element_type=F32)

        def static_bits(j):
            return [(j >> b) & 1 for b in range(bits)]

        def produce(k):
            cols = pl.ds(pl.multiple_of(z_of[k] * block, block), block)
            for j in range(half):
                value = project(j, cols, block).astype(BF16)
                for s in range(2):
                    grads[spot(s, z_of[k], static_bits(j))] = value[:, s * hd:(s + 1) * hd]

        if not stepwise:
            for j in range(half):
                value = project(j, pl.ds(0, chunk), chunk).astype(BF16)
                for zd in range(samples):
                    for s in range(2):
                        grads[spot(s, zd, static_bits(j))] = value[zd * block:(zd + 1) * block, s * hd:(s + 1) * hd]

        started = {}

        def kept(s, phase):
            fixed = [slice(None)] * bits
            for b in orders[s][:phase]:
                fixed[b] = my_bits[b]
            return fixed

        def send(k, phase):
            for s in range(2):
                b = orders[s][phase]
                fixed = kept(s, phase)
                fixed[b] = 1 - my_bits[b]
                c = remote(
                    grads.at[spot(s, z_of[k], fixed)], recv_bufs[s][phase].at[k],
                    red_send.at[s, phase, k], red_recv.at[s, phase, k], bit_peer[b])
                c.start()
                started[s, phase, k] = c

        def merge(k, phase):
            for s in range(2):
                started[s, phase, k].wait_recv()
                at = spot(s, z_of[k], kept(s, phase + 1))
                grads[at] = (grads[at].astype(F32) + recv_bufs[s][phase][k].astype(F32)).astype(BF16)

        z_copies = []

        def send_z(k):
            if k == 0:
                return
            for s in range(2):
                c = remote(
                    grads.at[spot(s, z_of[k], my_bits)], z_recv.at[s, k - 1],
                    z_send.at[s, k], z_recv_sem.at[s, k], z_peer[k])
                c.start()
                z_copies.append(c)

        steps = sorted(range(samples), key=lambda k: (-k.bit_length(), k))
        ahead = 1
        for tick in range(samples + ahead + bits):
            if tick < samples:
                if stepwise:
                    produce(steps[tick])
                send(steps[tick], 0)
            for phase in range(bits):
                at = tick - ahead - phase
                if 0 <= at < samples:
                    merge(steps[at], phase)
                    if phase + 1 < bits:
                        send(steps[at], phase + 1)
                    else:
                        send_z(steps[at])

        for c in prefix_copies:
            c.wait()
        own_sum = acc[own_rows, :hd] * scale
        own_val = acc[own_rows, hd:]
        for k in range(samples - 1):
            own_sum = own_sum + prefix_recv[k, :, :hd].astype(F32)
            own_val = own_val + prefix_recv[k, :, hd:].astype(F32)
        grad_prefix[0, :, :hd] = own_sum
        grad_prefix[0, :, hd:] = own_val

        for c in z_copies:
            c.wait()
        for s in range(2):
            value = grads[spot(s, z, my_bits)].astype(F32)
            for k in range(samples - 1):
                value = value + z_recv[s, k].astype(F32)
            grad_weight[:, s * hd:(s + 1) * hd] = value
        for c in started.values():
            c.wait_send()
        for c in out_copies:
            c.wait()

    keys = prefix + rows
    dma = pltpu.SemaphoreType.DMA
    reduce_bufs = [
        pltpu.VMEM((samples,) + (2,) * (bits - 1 - phase) + (block, hd), BF16)
        for _ in range(2) for phase in range(bits)
    ]
    scratch = [
        pltpu.VMEM((prompts, rows, chunk), BF16),
        pltpu.VMEM((half, rows, chunk), BF16),
        pltpu.VMEM((prompts, chunk, 2 * hd), BF16),
        pltpu.VMEM((rows, heads * hd), BF16),
        pltpu.VMEM((rows, heads * hd), BF16),
        pltpu.VMEM((keys, 2 * hd), BF16),
        pltpu.VMEM((2 * hd, keys), BF16),
        pltpu.VMEM((samples, 8, 128), F32),
        pltpu.VMEM((rows, heads * hd), F32),
        pltpu.VMEM((rows, heads * hd), F32),
        pltpu.VMEM((keys, 2 * hd), F32),
        pltpu.VMEM((prefix, 2 * hd), BF16),
        pltpu.VMEM((samples - 1, shard, 2 * hd), BF16),
        pltpu.VMEM((2, rows, 2 * hd), BF16),
        pltpu.VMEM((2, samples) + (2,) * bits + (block, hd), BF16),
        pltpu.VMEM((2, samples - 1, block, hd), BF16),
        pltpu.VMEM((heads, hd, rows), BF16),
        pltpu.VMEM((heads, rows, rows), F32),
        pltpu.VMEM((heads, rows, rows), F32),
        *reduce_bufs,
        dma((2 * prompts + 2,)), dma((2,)), dma((half,)), dma((half,)),
        dma((samples,)), dma((samples,)), dma((samples,)), dma((samples,)),
        dma, dma, dma, dma((samples,)), dma((samples,)),
        dma((2, bits, samples)), dma((2, bits, samples)), dma((2, samples)), dma((2, samples)),
    ]
    anywhere = pl.BlockSpec(memory_space=pl.ANY)
    smem = pl.BlockSpec(memory_space=pltpu.SMEM)
    vmem = pl.BlockSpec(memory_space=pltpu.VMEM)
    flops = 4 * rows * model * 2 * hd + 14 * rows * heads * keys * hd
    return pl.pallas_call(
        kernel,
        out_shape=(
            jax.ShapeDtypeStruct((1, 1, rows, heads * hd), F32),
            jax.ShapeDtypeStruct((1, 1, rows, heads * hd), F32),
            jax.ShapeDtypeStruct((1, shard, 2 * hd), F32),
            jax.ShapeDtypeStruct((block, 2 * hd), F32),
        ),
        in_specs=[anywhere] * 5 + [smem] * 2,
        out_specs=(anywhere, anywhere, vmem, vmem),
        scratch_shapes=scratch,
        compiler_params=pltpu.CompilerParams(
            collective_id=0, has_side_effects=True, vmem_limit_bytes=56 * 1024 * 1024),
        cost_estimate=pl.CostEstimate(
            flops=flops, bytes_accessed=16 * 1024 * 1024, transcendentals=rows * heads * keys),
    )


def hand_out(arrays, pieces=2):
    def kernel(*refs):
        count = len(arrays)
        ins, outs, held, sem = refs[:count], refs[count:2 * count], refs[2 * count:3 * count], refs[3 * count]
        loads, stores = [], []
        for i in range(count):
            axis = len(ins[i].shape) - 2
            step = ins[i].shape[axis] // pieces
            for j in range(pieces):
                at = (0,) * axis + (pl.ds(j * step, step),)
                loads.append(pltpu.make_async_copy(ins[i].at[at], held[i].at[at], sem.at[0, i, j]))
                stores.append(pltpu.make_async_copy(held[i].at[at], outs[i].at[at], sem.at[1, i, j]))
        for c in loads:
            c.start()
        for load, store in zip(loads, stores):
            load.wait()
            store.start()
        for c in stores:
            c.wait()

    anywhere = pl.BlockSpec(memory_space=pl.ANY)
    size = sum(a.size * 4 for a in arrays)
    return pl.pallas_call(
        kernel,
        out_shape=tuple(jax.ShapeDtypeStruct(a.shape, a.dtype) for a in arrays),
        in_specs=[anywhere] * len(arrays),
        out_specs=(anywhere,) * len(arrays),
        scratch_shapes=[pltpu.VMEM(a.shape, a.dtype) for a in arrays]
        + [pltpu.SemaphoreType.DMA((2, len(arrays), pieces))],
        compiler_params=pltpu.CompilerParams(vmem_limit_bytes=60 * 1024 * 1024),
        cost_estimate=pl.CostEstimate(flops=0, bytes_accessed=2 * size, transcendentals=0),
    )(*arrays)


def solution(mesh):
    prompts, samples = mesh.shape["prompt"], mesh.shape["resp"]

    def on_device(hidden, queries, prefix_kv, weight, out_grad, lengths, rewards):
        hd = weight.shape[1] // 2
        call = make_kernel(
            prompts, samples, hidden.shape[2], queries.shape[3] // hd, hd, prefix_kv.shape[1], weight.shape[0])
        return tuple(hand_out(call(hidden, queries, prefix_kv, weight, out_grad, lengths, rewards)))

    placed = P("prompt", "resp", None, None)
    return jax.shard_map(
        on_device,
        mesh=mesh,
        in_specs=(placed, placed, P("prompt", "resp", None), P(), placed, P("prompt", "resp"), P("prompt", "resp")),
        out_specs=(placed, placed, P("prompt", "resp", None), P(("prompt", "resp"), None)),
        check_vma=False,
    )
```
